32 devices in a mesh: blk: 16 (over z, y, core), rows: 2 (over x).
Axes of the slice: x: 2, y: 2, z: 4, core: 2. Of those that a mesh axis runs over, the one named last changes fastest.
Arguments:
- tokens: bfloat16 [64, 8192], P(('blk', 'rows')), may hold values from -60 to 60
- norm_gain: float32 [8192], replicated, may hold values from 0.1 to 1.9
- gate_weight: bfloat16 [8192, 4096], P(None, 'blk'), may hold values from -0.09375 to 0.09375
- up_weight: bfloat16 [8192, 4096], P(None, 'blk'), may hold values from -0.09375 to 0.09375
- down_weight: bfloat16 [4096, 8192], P('blk'), may hold values from -0.125 to 0.125
- gate_mask: int32 [64, 32], P(None, 'blk'), may hold values from 0 to 1, as said below
- up_mask: int32 [64, 32], P(None, 'blk'), may hold values from 0 to 1, as said below
- down_mask: int32 [32, 64], P('blk'), may hold values 0 or 1
Outputs:
- ffn_out: bfloat16 [64, 8192], P(('blk', 'rows'))
The draws below stay inside these ranges and needn't reach their ends.
Inputs may be any that keep to these rules, and one draw needn't show every extreme that they name: Each column of gate_mask (64 block flags) has between 16 and 48 ones, and some column has exactly 48. Each column of up_mask (64 block flags) has between 16 and 48 ones, and some column has exactly 48.
All inputs are finite; a program needn't handle non-finite values. No bound on the sum of `down_mask` on one device may be relied on, other than what follows from the above.
Results may differ from the reference program's by a relative error of at most 0.0065.
Values may be sent and summed in bfloat16 or wider, within the bound.
A program may use at most 128 MiB of HBM per device.

```python
import math
import jax
import jax.numpy as jnp
from jax import lax

D = 8192
PANEL = 256
FF = 4096
BLOCK = 128
RB = 64
FB = 32
KEEP_LEAST = 16
KEEP_MOST = 48
TOKENS = 64


def draw_tokens(key, part):
    key_base, key_rows, key_cols = jax.random.split(key, 3)
    row_scale = jnp.exp(jax.random.uniform(key_rows, (TOKENS, 1), jnp.float32, math.log(0.3), math.log(3.0)))
    col_scale = jnp.exp(jax.random.uniform(key_cols, (1, D), jnp.float32, math.log(0.3), math.log(3.0)))
    base = jnp.clip(jax.random.normal(key_base, (TOKENS, D), jnp.float32), -6.0, 6.0)
    return (base * row_scale * col_scale).astype(jnp.bfloat16)


def block_flags(key):
    key_count, key_which, key_score = jax.random.split(key, 3)
    counts = jax.random.randint(key_count, (FB,), KEEP_LEAST, KEEP_MOST + 1)
    which = jax.random.randint(key_which, (), 0, FB)
    counts = jnp.where(jnp.arange(FB) == which, KEEP_MOST, counts)
    scores = jax.random.randint(key_score, (RB, FB), 0, 1 << 20) * RB + jnp.arange(RB)[:, None]
    ranks = jnp.argsort(jnp.argsort(scores, axis=0), axis=0)
    return (ranks < counts[None, :]).astype(jnp.int32)


def draw_gate_mask(key, part):
    return block_flags(jax.random.fold_in(key, 11))


def draw_up_mask(key, part):
    return block_flags(jax.random.fold_in(key, 23))


def with_ends(result, key, smallest, largest):
    longest = result.shape.index(max(result.shape))
    spots = []
    for shift in (0, 1):
        where = [jax.random.randint(jax.random.fold_in(key, axis), (), 0, length) for axis, length in enumerate(result.shape)]
        where[longest] = (where[longest] + shift) % result.shape[longest]
        spots.append(tuple(where))
    return result.at[spots[0]].set(smallest).at[spots[1]].set(largest)


def shard_levels(own_key, dims, pieces, smallest, high):
    def one(position, shards_of):
        steps = jax.random.uniform(jax.random.fold_in(jax.random.fold_in(own_key, 6), position), (shards_of,), jnp.float32, smallest / len(pieces), high / len(pieces))
        return jnp.repeat(jnp.exp(steps), dims[position] // shards_of).reshape((-1,) + (1,) * (len(dims) - position - 1))

    level = one(*pieces[0])
    for cut in pieces[1:]:
        level = level * one(*cut)
    return level


def centred(stream_key, dims, scale, reach, cuts=(), held_as=jnp.bfloat16):
    loudness = shard_levels(stream_key, dims, cuts, -0.22, 0.18) if cuts else 1.0
    result = jax.random.normal(stream_key, dims, jnp.float32) * scale * loudness
    return jnp.minimum(jnp.maximum(result, -reach), reach).astype(held_as)


def setup_inputs(seed: int = 0) -> dict:
    keys = jax.random.split(jax.random.key(seed), 9)
    tokens = draw_tokens(jax.random.fold_in(keys[8], 71), 0)
    norm_gain = jnp.clip(1.0 + 0.18 * jax.random.normal(keys[1], (D,), jnp.float32), 0.1, 1.9)
    gate_weight = centred(keys[2], (D, FF), (D // 2) ** -0.5, 0.09375, ((1, 16),))
    up_weight = centred(keys[3], (D, FF), (D // 2) ** -0.5, 0.09375, ((1, 16),))
    down_weight = centred(keys[4], (FF, D), (FF // 2) ** -0.5, 0.125, ((0, 16),))
    gate_mask = draw_gate_mask(jax.random.fold_in(keys[8], 71), 0)
    up_mask = draw_up_mask(jax.random.fold_in(keys[8], 71), 0)
    down_mask = with_ends((jax.random.randint(keys[7], (FB, RB), 0, 2) < 1).astype(jnp.int32), jax.random.fold_in(keys[7], 1), 0, 1)
    return dict(tokens=tokens, norm_gain=norm_gain, gate_weight=gate_weight, up_weight=up_weight, down_weight=down_weight, gate_mask=gate_mask, up_mask=up_mask, down_mask=down_mask)


def mask_blocks(weight, flags):
    height, width = weight.shape
    down_n = flags.shape[0]
    across_n = flags.shape[1]
    shaped = weight.reshape(down_n, height // down_n, across_n, width // across_n)
    return (shaped * flags.astype(weight.dtype)[:, None, :, None]).reshape(height, width)

def reference(tokens, norm_gain, gate_weight, up_weight, down_weight, gate_mask, up_mask, down_mask):
    wide_tok = tokens.astype(jnp.float32)
    scale_inv = lax.rsqrt(lax.optimization_barrier(jnp.mean(wide_tok * wide_tok, axis=-1, keepdims=True)) + 1e-05)
    normed = (wide_tok * scale_inv * norm_gain.astype(jnp.float32)).astype(jnp.bfloat16)
    flag_cols = PANEL // BLOCK

    def one_panel(index, total):
        panel_at = jnp.asarray(index).astype(jnp.int32) * PANEL
        flag_at = jnp.asarray(index).astype(jnp.int32) * flag_cols
        gate_part = mask_blocks(lax.dynamic_slice_in_dim(gate_weight, panel_at, PANEL, 1), lax.dynamic_slice_in_dim(gate_mask, flag_at, flag_cols, 1))
        up_part = mask_blocks(lax.dynamic_slice_in_dim(up_weight, panel_at, PANEL, 1), lax.dynamic_slice_in_dim(up_mask, flag_at, flag_cols, 1))
        down_part = mask_blocks(lax.dynamic_slice_in_dim(down_weight, panel_at, PANEL, 0), lax.dynamic_slice_in_dim(down_mask, flag_at, flag_cols, 0))
        gate = jnp.dot(normed, gate_part, preferred_element_type=jnp.float32)
        up_val = jnp.dot(normed, up_part, preferred_element_type=jnp.float32)
        hidden = (jax.nn.silu(gate) * up_val).astype(jnp.bfloat16)
        return total + jnp.dot(hidden, down_part, preferred_element_type=jnp.float32)
    start_sum = jnp.zeros((tokens.shape[0], tokens.shape[1]), jnp.float32)
    total = lax.fori_loop(0, FF // PANEL, one_panel, start_sum)
    return total.astype(jnp.bfloat16)
```

```python
import functools

import jax
import jax.numpy as jnp
from jax import lax
from jax.experimental import pallas as pl
from jax.experimental.pallas import tpu as pltpu
from jax.sharding import PartitionSpec as P

MESH = pl.DeviceIdType.MESH
F32 = jnp.float32
BF16 = jnp.bfloat16
LANES = 128
CUT = 1024
GROUP = 16


def permutation(to_tokens):
    size = GROUP * 16
    row = lax.broadcasted_iota(jnp.int32, (size, size), 0)
    col = lax.broadcasted_iota(jnp.int32, (size, size), 1)
    if not to_tokens:
        row, col = col, row
    block, device, token = row >> 5, (row & 31) >> 1, row & 1
    return jnp.where(device * 16 + block * 2 + token == col, 1.0, 0.0).astype(BF16)


def kernel(
    nblk,
    tok_ref,
    gain_ref,
    gm_ref,
    um_ref,
    dm_ref,
    wg_hbm,
    wu_hbm,
    wd_hbm,
    out_ref,
    wg,
    wu,
    wd,
    wide,
    slabs,
    x,
    swap_out,
    swap_in,
    rs_out,
    rs_in,
    fin_out,
    fin_in,
    w_sem,
    ag_send,
    fw_send,
    ag_recv,
    swap_send,
    swap_recv,
    rs_send,
    rs_recv,
    fin_send,
    fin_recv,
):
    nchips = nblk // 2
    feats = wg.shape[0]
    hid = wg.shape[1]
    blocks = feats // LANES
    cuts = feats // CUT
    half_cuts = cuts // 2
    rows_half = blocks
    groups = nblk // GROUP
    me = lax.axis_index("blk")
    chip, core = me // 2, me % 2
    sib = chip * 2 + (1 - core)

    def peer(o):
        return lax.rem(chip + o, nchips)

    loads = []
    for n in range(4):
        r = feats // 4
        rs = pl.ds(n * r, r)
        loads.append(
            (
                pltpu.make_async_copy(wg_hbm.at[rs], wg.at[rs], w_sem.at[0, n]),
                pltpu.make_async_copy(wu_hbm.at[rs], wu.at[rs], w_sem.at[1, n]),
            )
        )
    down_loads = []
    for n in range(4):
        r = feats // 4
        cs = pl.ds(n * r, r)
        down_loads.append(pltpu.make_async_copy(wd_hbm.at[:, cs], wd.at[:, cs], w_sem.at[2, n]))
    for a, b in loads:
        a.start()
        b.start()
    for a in down_loads:
        a.start()

    barrier = pltpu.get_barrier_semaphore()
    pl.semaphore_signal(barrier, inc=1, device_id={"blk": sib}, device_id_type=MESH)

    def greet(o, c):
        pl.semaphore_signal(barrier, inc=1, device_id={"blk": peer(o) * 2 + core}, device_id_type=MESH)
        return c

    lax.fori_loop(1, nchips, greet, 0)

    tok = tok_ref[...].astype(F32)
    inv = lax.rsqrt(jnp.mean(tok * tok, axis=-1, keepdims=True) + 1e-05)
    normed = tok * inv * gain_ref[...]
    for b in range(blocks):
        wide[pl.ds(2 * b, 2), :] = normed[:, b * LANES : (b + 1) * LANES]
    slabs[me] = wide[...].astype(BF16)

    pl.semaphore_wait(barrier, nchips)

    def ag_copy(src, dev, send):
        return pltpu.make_async_remote_copy(
            src_ref=slabs.at[src],
            dst_ref=slabs.at[src],
            send_sem=send,
            recv_sem=ag_recv.at[src],
            device_id={"blk": dev},
            device_id_type=MESH,
        )

    def send_all(o, c):
        ag_copy(me, peer(o) * 2 + core, ag_send.at[o]).start()
        return c

    lax.fori_loop(1, nchips, send_all, 0)
    ag_copy(me, sib, ag_send.at[0]).start()

    def flagged(w, flag):
        keep = jnp.broadcast_to(flag.astype(F32), (16, LANES)).astype(BF16)
        return (w.reshape(8, 16, LANES) * keep[None]).reshape(LANES, LANES)

    per = blocks // 4
    for n in range(4):
        loads[n][0].wait()
        loads[n][1].wait()

        def mask_in(i, c):
            i = n * per + i
            rs = pl.ds(pl.multiple_of(i * LANES, LANES), LANES)
            for j in range(hid // LANES):
                cs = pl.ds(j * LANES, LANES)
                wg[rs, cs] = flagged(wg[rs, cs], gm_ref[i, j])
                wu[rs, cs] = flagged(wu[rs, cs], um_ref[i, j])
            return c

        lax.fori_loop(0, per, mask_in, 0)

    def forward(o, c):
        src = lax.rem(chip + nchips - o, nchips) * 2 + core
        ag_copy(src, sib, fw_send.at[o]).wait_recv()
        ag_copy(src, sib, fw_send.at[o]).start()
        return c

    lax.fori_loop(1, nchips, forward, 0)

    for n in range(4):
        down_loads[n].wait()

        def mask_down(i, c):
            i = n * per + i
            cs = pl.ds(pl.multiple_of(i * LANES, LANES), LANES)
            for j in range(hid // LANES):
                rs = pl.ds(j * LANES, LANES)
                wd[rs, cs] = flagged(wd[rs, cs], dm_ref[j, i])
            return c

        lax.fori_loop(0, per, mask_down, 0)

    def arrived(o, c):
        src = lax.rem(chip + nchips - o, nchips) * 2 + (1 - core)
        ag_copy(src, sib, fw_send.at[0]).wait_recv()
        return c

    lax.fori_loop(0, nchips, arrived, 0)

    to_tokens = permutation(True)
    gate = jnp.zeros((2 * nblk, hid), F32)
    up = jnp.zeros((2 * nblk, hid), F32)
    for n in range(cuts):
        for g in range(groups):
            part = slabs[pl.ds(g * GROUP, GROUP), pl.ds(n * 16, 16), :].reshape(GROUP * 16, LANES)
            turned = jnp.dot(to_tokens, part, preferred_element_type=F32).astype(BF16)
            for b in range(8):
                x[pl.ds(g * 32, 32), pl.ds(b * LANES, LANES)] = turned[b * 32 : (b + 1) * 32]
        rs = pl.ds(n * CUT, CUT)
        gate = gate + jnp.dot(x[...], wg[rs, :], preferred_element_type=F32)
        up = up + jnp.dot(x[...], wu[rs, :], preferred_element_type=F32)
    hidden = (gate / (1.0 + jnp.exp(-gate)) * up).astype(BF16)

    def swap_copy(n):
        cs = pl.ds(n * CUT, CUT)
        return pltpu.make_async_remote_copy(
            src_ref=swap_out.at[:, cs],
            dst_ref=swap_in.at[:, cs],
            send_sem=swap_send.at[n],
            recv_sem=swap_recv.at[n],
            device_id={"blk": sib},
            device_id_type=MESH,
        )

    for n in range(half_cuts):
        at = pl.multiple_of(((1 - core) * half_cuts + n) * CUT, CUT)
        part = jnp.dot(hidden, wd[:, pl.ds(at, CUT)], preferred_element_type=F32)
        swap_out[:, pl.ds(n * CUT, CUT)] = part.astype(BF16)
        swap_copy(n).start()

    to_slabs = permutation(False)
    for n in range(half_cuts):
        at = pl.multiple_of((core * half_cuts + n) * CUT, CUT)
        part = jnp.dot(hidden, wd[:, pl.ds(at, CUT)], preferred_element_type=F32)
        swap_copy(n).wait_recv()
        both = (part + swap_in[:, pl.ds(n * CUT, CUT)].astype(F32)).astype(BF16)
        for g in range(groups):
            mine = both[g * 32 : (g + 1) * 32]
            stacked = jnp.concatenate([mine[:, b * LANES : (b + 1) * LANES] for b in range(8)], axis=0)
            turned = jnp.dot(to_slabs, stacked, preferred_element_type=F32).astype(BF16)
            rs_out[pl.ds(g * GROUP // 2, GROUP // 2), :, pl.ds(n * 16, 16), :] = turned.reshape(
                GROUP // 2, 2, 16, LANES
            )

    def rs_copy(src, dst, o, dev):
        return pltpu.make_async_remote_copy(
            src_ref=rs_out.at[src],
            dst_ref=rs_in.at[dst],
            send_sem=rs_send.at[o],
            recv_sem=rs_recv.at[dst],
            device_id={"blk": dev},
            device_id_type=MESH,
        )

    def rs_start(o, c):
        to = peer(o)
        rs_copy(to, chip, o, to * 2 + core).start()
        return c

    lax.fori_loop(1, nchips, rs_start, 0)

    def rs_add(o, total):
        src = lax.rem(chip + nchips - o, nchips)
        rs_copy(src, src, o, src * 2 + core).wait_recv()
        return total + rs_in[src].astype(F32)

    total = lax.fori_loop(1, nchips, rs_add, rs_out[chip].astype(F32))
    fin_out[...] = total.astype(BF16)
    fin = pltpu.make_async_remote_copy(
        src_ref=fin_out.at[1 - core],
        dst_ref=fin_in,
        send_sem=fin_send,
        recv_sem=fin_recv,
        device_id={"blk": sib},
        device_id_type=MESH,
    )
    fin.start()
    out_ref[core] = fin_out[core]

    def drain(o, c):
        ag_copy(me, sib, ag_send.at[o]).wait_send()
        ag_copy(me, sib, fw_send.at[o]).wait_send()
        rs_copy(chip, chip, o, sib).wait_send()
        return c

    lax.fori_loop(1, nchips, drain, 0)
    ag_copy(me, sib, ag_send.at[0]).wait_send()
    for n in range(half_cuts):
        swap_copy(n).wait_send()
    fin.wait()
    out_ref[1 - core] = fin_in[...]


def local(nblk, tokens, norm_gain, gate_weight, up_weight, down_weight, gate_mask, up_mask, down_mask):
    own, feats = tokens.shape
    hid = gate_weight.shape[1]
    blocks = feats // LANES
    half = feats // 2
    nchips = nblk // 2
    cuts = half // CUT
    vmem = pl.BlockSpec(memory_space=pltpu.VMEM)
    smem = pl.BlockSpec(memory_space=pltpu.SMEM)
    anyw = pl.BlockSpec(memory_space=pl.ANY)
    dma = pltpu.SemaphoreType.DMA
    out = pl.pallas_call(
        functools.partial(kernel, nblk),
        out_shape=jax.ShapeDtypeStruct((2, blocks, LANES), BF16),
        in_specs=[vmem, vmem, smem, smem, smem, anyw, anyw, anyw],
        out_specs=vmem,
        scratch_shapes=[
            pltpu.VMEM((feats, hid), BF16),
            pltpu.VMEM((feats, hid), BF16),
            pltpu.VMEM((hid, feats), BF16),
            pltpu.VMEM((2 * blocks, LANES), F32),
            pltpu.VMEM((nblk, 2 * blocks, LANES), BF16),
            pltpu.VMEM((2 * nblk, CUT), BF16),
            pltpu.VMEM((2 * nblk, half), BF16),
            pltpu.VMEM((2 * nblk, half), BF16),
            pltpu.VMEM((nchips, 2, blocks, LANES), BF16),
            pltpu.VMEM((nchips, 2, blocks, LANES), BF16),
            pltpu.VMEM((2, blocks, LANES), BF16),
            pltpu.VMEM((blocks, LANES), BF16),
            dma((3, 4)),
            dma((nchips,)),
            dma((nchips,)),
            dma((nblk,)),
            dma((cuts,)),
            dma((cuts,)),
            dma((nchips,)),
            dma((nchips,)),
            dma,
            dma,
        ],
        compiler_params=pltpu.CompilerParams(
            collective_id=0, has_side_effects=True, vmem_limit_bytes=50 * 1024 * 1024
        ),
    )(
        tokens,
        norm_gain.reshape(1, feats),
        gate_mask,
        up_mask,
        down_mask,
        gate_weight,
        up_weight,
        down_weight,
    )
    return out.reshape(blocks, 2, LANES).transpose(1, 0, 2).reshape(own, feats)


def solution(mesh):
    return jax.shard_map(
        functools.partial(local, mesh.shape["blk"]),
        mesh=mesh,
        in_specs=(
            P(("blk", "rows"), None),
            P(),
            P(None, "blk"),
            P(None, "blk"),
            P("blk", None),
            P(None, "blk"),
            P(None, "blk"),
            P("blk", None),
        ),
        out_specs=P(("blk", "rows"), None),
        check_vma=False,
    )
```

```python
import functools

import jax
import jax.numpy as jnp
from jax import lax
from jax.experimental import pallas as pl
from jax.experimental.pallas import tpu as pltpu
from jax.sharding import PartitionSpec as P

MESH = pl.DeviceIdType.MESH
F32 = jnp.float32
BF16 = jnp.bfloat16
LANES = 128
CUT = 1024
GROUP = 16


def permutation(to_tokens):
    size = GROUP * 16
    row = lax.broadcasted_iota(jnp.int32, (size, size), 0)
    col = lax.broadcasted_iota(jnp.int32, (size, size), 1)
    if not to_tokens:
        row, col = col, row
    block, device, token = row >> 5, (row & 31) >> 1, row & 1
    return jnp.where(device * 16 + block * 2 + token == col, 1.0, 0.0).astype(BF16)


def kernel(
    nblk,
    tok_hbm,
    gain_hbm,
    gm_hbm,
    um_hbm,
    dm_hbm,
    wg_hbm,
    wu_hbm,
    wd_hbm,
    out_ref,
    tok_ref,
    gain_ref,
    gm_ref,
    um_ref,
    dm_ref,
    wg,
    wu,
    wd,
    wide,
    slabs,
    x,
    swap_out,
    swap_in,
    rs_out,
    rs_in,
    fin_out,
    fin_in,
    s_sem,
    w_sem,
    ag_send,
    by_send,
    fw_send,
    ag_recv,
    swap_send,
    swap_recv,
    rs_send,
    rs_recv,
    fin_send,
    fin_recv,
):
    nchips = nblk // 2
    feats = wg.shape[0]
    hid = wg.shape[1]
    blocks = feats // LANES
    cuts = feats // CUT
    half_cuts = cuts // 2
    rows_half = blocks
    groups = nblk // GROUP
    me = lax.axis_index("blk")
    chip, core = me // 2, me % 2
    sib = chip * 2 + (1 - core)

    def peer(o):
        return lax.rem(chip + o, nchips)

    smalls = [
        pltpu.make_async_copy(a, b, s_sem.at[n])
        for n, (a, b) in enumerate(
            (
                (tok_hbm, tok_ref),
                (gain_hbm, gain_ref),
                (gm_hbm, gm_ref),
                (um_hbm, um_ref),
                (dm_hbm, dm_ref),
            )
        )
    ]
    for a in smalls:
        a.start()

    loads = []
    for n in range(4):
        r = feats // 4
        rs = pl.ds(n * r, r)
        loads.append(
            (
                pltpu.make_async_copy(wg_hbm.at[rs], wg.at[rs], w_sem.at[0, n]),
                pltpu.make_async_copy(wu_hbm.at[rs], wu.at[rs], w_sem.at[1, n]),
            )
        )
    down_loads = []
    for n in range(4):
        r = feats // 4
        cs = pl.ds(n * r, r)
        down_loads.append(pltpu.make_async_copy(wd_hbm.at[:, cs], wd.at[:, cs], w_sem.at[2, n]))
    for a, b in loads:
        a.start()
        b.start()
    for a in down_loads:
        a.start()

    barrier = pltpu.get_barrier_semaphore()
    pl.semaphore_signal(barrier, inc=1, device_id={"blk": sib}, device_id_type=MESH)

    def greet(o, c):
        pl.semaphore_signal(barrier, inc=1, device_id={"blk": peer(o) * 2 + core}, device_id_type=MESH)
        return c

    lax.fori_loop(1, nchips, greet, 0)

    smalls[0].wait()
    smalls[1].wait()
    tok = tok_ref[...].astype(F32)
    inv = lax.rsqrt(jnp.mean(tok * tok, axis=-1, keepdims=True) + 1e-05)
    normed = tok * inv * gain_ref[...]
    for b in range(blocks):
        wide[pl.ds(2 * b, 2), :] = normed[:, b * LANES : (b + 1) * LANES]
    slabs[me] = wide[...].astype(BF16)

    pl.semaphore_wait(barrier, nchips)

    def ag_copy(src, dev, send):
        return pltpu.make_async_remote_copy(
            src_ref=slabs.at[src],
            dst_ref=slabs.at[src],
            send_sem=send,
            recv_sem=ag_recv.at[src],
            device_id={"blk": dev},
            device_id_type=MESH,
        )

    pairs = nchips // 2
    pair, side = chip // 2, chip % 2
    beside = (pair * 2 + (1 - side)) * 2 + core

    def slab_of(o, s, c):
        return (lax.rem(pair + pairs - o, pairs) * 2 + s) * 2 + c

    def send_all(o, c):
        ag_copy(me, (lax.rem(pair + o, pairs) * 2 + side) * 2 + core, ag_send.at[o]).start()
        return c

    lax.fori_loop(1, pairs, send_all, 0)
    ag_copy(me, beside, by_send.at[0]).start()
    ag_copy(me, sib, fw_send.at[0, 0]).start()
    for a in smalls[2:]:
        a.wait()

    def forward_both(o, c):
        src = slab_of(o, side, core)
        ag_copy(src, sib, fw_send.at[0, o]).wait_recv()
        ag_copy(src, beside, by_send.at[o]).start()
        ag_copy(src, sib, fw_send.at[0, o]).start()
        return c

    def forward_last(o, c):
        src = slab_of(o, 1 - side, core)
        ag_copy(src, sib, fw_send.at[1, o]).wait_recv()
        ag_copy(src, sib, fw_send.at[1, o]).start()
        return c

    def flagged(w, flag):
        keep = jnp.broadcast_to(flag.astype(F32), (16, LANES)).astype(BF16)
        return (w.reshape(8, 16, LANES) * keep[None]).reshape(LANES, LANES)

    per = blocks // 4
    for n in range(4):
        loads[n][0].wait()
        loads[n][1].wait()

        def mask_in(i, c):
            i = n * per + i
            rs = pl.ds(pl.multiple_of(i * LANES, LANES), LANES)
            for j in range(hid // LANES):
                cs = pl.ds(j * LANES, LANES)
                wg[rs, cs] = flagged(wg[rs, cs], gm_ref[j, i])
                wu[rs, cs] = flagged(wu[rs, cs], um_ref[j, i])
            return c

        lax.fori_loop(0, per, mask_in, 0)
        lax.fori_loop(1 + (pairs - 1) * n // 4, 1 + (pairs - 1) * (n + 1) // 4, forward_both, 0)

    for n in range(4):
        down_loads[n].wait()

        def mask_down(i, c):
            i = n * per + i
            cs = pl.ds(pl.multiple_of(i * LANES, LANES), LANES)
            for j in range(hid // LANES):
                rs = pl.ds(j * LANES, LANES)
                wd[rs, cs] = flagged(wd[rs, cs], dm_ref[j, i])
            return c

        lax.fori_loop(0, per, mask_down, 0)
        lax.fori_loop(pairs * n // 4, pairs * (n + 1) // 4, forward_last, 0)

    def arrived(o, c):
        src = lax.rem(chip + nchips - o, nchips) * 2 + (1 - core)
        ag_copy(src, sib, fw_send.at[0, 0]).wait_recv()
        return c

    lax.fori_loop(0, nchips, arrived, 0)

    to_tokens = permutation(True)
    gate = jnp.zeros((2 * nblk, hid), F32)
    up = jnp.zeros((2 * nblk, hid), F32)
    for n in range(cuts):
        for g in range(groups):
            part = slabs[pl.ds(g * GROUP, GROUP), pl.ds(n * 16, 16), :].reshape(GROUP * 16, LANES)
            turned = jnp.dot(to_tokens, part, preferred_element_type=F32).astype(BF16)
            for b in range(8):
                x[pl.ds(g * 32, 32), pl.ds(b * LANES, LANES)] = turned[b * 32 : (b + 1) * 32]
        rs = pl.ds(n * CUT, CUT)
        gate = gate + jnp.dot(x[...], wg[rs, :], preferred_element_type=F32)
        up = up + jnp.dot(x[...], wu[rs, :], preferred_element_type=F32)
    hidden = (gate / (1.0 + jnp.exp(-gate)) * up).astype(BF16)

    def swap_copy(n):
        cs = pl.ds(n * CUT, CUT)
        return pltpu.make_async_remote_copy(
            src_ref=swap_out.at[:, cs],
            dst_ref=swap_in.at[:, cs],
            send_sem=swap_send.at[n],
            recv_sem=swap_recv.at[n],
            device_id={"blk": sib},
            device_id_type=MESH,
        )

    for n in range(half_cuts):
        at = pl.multiple_of(((1 - core) * half_cuts + n) * CUT, CUT)
        part = jnp.dot(hidden, wd[:, pl.ds(at, CUT)], preferred_element_type=F32)
        swap_out[:, pl.ds(n * CUT, CUT)] = part.astype(BF16)
        swap_copy(n).start()

    def rs_copy(src, dst, o, dev, n):
        rows = pl.ds(n * 16, 16)
        return pltpu.make_async_remote_copy(
            src_ref=rs_out.at[src, :, rows],
            dst_ref=rs_in.at[dst, :, rows],
            send_sem=rs_send.at[o, n],
            recv_sem=rs_recv.at[dst, n],
            device_id={"blk": dev},
            device_id_type=MESH,
        )

    to_slabs = permutation(False)
    for n in range(half_cuts):
        at = pl.multiple_of((core * half_cuts + n) * CUT, CUT)
        part = jnp.dot(hidden, wd[:, pl.ds(at, CUT)], preferred_element_type=F32)
        swap_copy(n).wait_recv()
        both = (part + swap_in[:, pl.ds(n * CUT, CUT)].astype(F32)).astype(BF16)
        for g in range(groups):
            mine = both[g * 32 : (g + 1) * 32]
            stacked = jnp.concatenate([mine[:, b * LANES : (b + 1) * LANES] for b in range(8)], axis=0)
            turned = jnp.dot(to_slabs, stacked, preferred_element_type=F32).astype(BF16)
            rs_out[pl.ds(g * GROUP // 2, GROUP // 2), :, pl.ds(n * 16, 16), :] = turned.reshape(
                GROUP // 2, 2, 16, LANES
            )

        def rs_start(o, c):
            to = peer(o)
            rs_copy(to, chip, o, to * 2 + core, n).start()
            return c

        lax.fori_loop(1, nchips, rs_start, 0)

    def rs_add(o, total):
        src = lax.rem(chip + nchips - o, nchips)
        for n in range(half_cuts):
            rs_copy(src, src, o, src * 2 + core, n).wait_recv()
        return total + rs_in[src].astype(F32)

    total = lax.fori_loop(1, nchips, rs_add, rs_out[chip].astype(F32))
    fin_out[...] = total.astype(BF16)
    fin = pltpu.make_async_remote_copy(
        src_ref=fin_out.at[1 - core],
        dst_ref=fin_in,
        send_sem=fin_send,
        recv_sem=fin_recv,
        device_id={"blk": sib},
        device_id_type=MESH,
    )
    fin.start()
    out_ref[core] = fin_out[core]

    def drain_own(o, c):
        ag_copy(me, sib, ag_send.at[o]).wait_send()
        return c

    def drain_forwards(o, c):
        ag_copy(me, sib, by_send.at[o]).wait_send()
        ag_copy(me, sib, fw_send.at[0, o]).wait_send()
        ag_copy(me, sib, fw_send.at[1, o]).wait_send()
        return c

    def drain_sums(o, c):
        for n in range(half_cuts):
            rs_copy(chip, chip, o, sib, n).wait_send()
        return c

    lax.fori_loop(1, pairs, drain_own, 0)
    lax.fori_loop(0, pairs, drain_forwards, 0)
    lax.fori_loop(1, nchips, drain_sums, 0)
    for n in range(half_cuts):
        swap_copy(n).wait_send()
    fin.wait()
    out_ref[1 - core] = fin_in[...]


def local(nblk, tokens, norm_gain, gate_weight, up_weight, down_weight, gate_mask, up_mask, down_mask):
    own, feats = tokens.shape
    hid = gate_weight.shape[1]
    blocks = feats // LANES
    half = feats // 2
    nchips = nblk // 2
    cuts = half // CUT
    vmem = pl.BlockSpec(memory_space=pltpu.VMEM)
    held = pl.BlockSpec(memory_space=pltpu.HBM)
    anyw = pl.BlockSpec(memory_space=pl.ANY)
    dma = pltpu.SemaphoreType.DMA
    out = pl.pallas_call(
        functools.partial(kernel, nblk),
        out_shape=jax.ShapeDtypeStruct((2, blocks, LANES), BF16),
        in_specs=[held] * 5 + [anyw] * 3,
        out_specs=vmem,
        scratch_shapes=[
            pltpu.VMEM((own, feats), BF16),
            pltpu.VMEM((1, feats), F32),
            pltpu.SMEM((hid // LANES, blocks), jnp.int32),
            pltpu.SMEM((hid // LANES, blocks), jnp.int32),
            pltpu.SMEM((hid // LANES, blocks), jnp.int32),
            pltpu.VMEM((feats, hid), BF16),
            pltpu.VMEM((feats, hid), BF16),
            pltpu.VMEM((hid, feats), BF16),
            pltpu.VMEM((2 * blocks, LANES), F32),
            pltpu.VMEM((nblk, 2 * blocks, LANES), BF16),
            pltpu.VMEM((2 * nblk, CUT), BF16),
            pltpu.VMEM((2 * nblk, half), BF16),
            pltpu.VMEM((2 * nblk, half), BF16),
            pltpu.VMEM((nchips, 2, blocks, LANES), BF16),
            pltpu.VMEM((nchips, 2, blocks, LANES), BF16),
            pltpu.VMEM((2, blocks, LANES), BF16),
            pltpu.VMEM((blocks, LANES), BF16),
            dma((5,)),
            dma((3, 4)),
            dma((nchips // 2,)),
            dma((nchips // 2,)),
            dma((2, nchips // 2)),
            dma((nblk,)),
            dma((cuts,)),
            dma((cuts,)),
            dma((nchips, cuts)),
            dma((nchips, cuts)),
            dma,
            dma,
        ],
        compiler_params=pltpu.CompilerParams(
            collective_id=0, has_side_effects=True, vmem_limit_bytes=64 * 1024 * 1024 - 65536
        ),
    )(
        tokens,
        norm_gain.reshape(1, feats),
        gate_mask.T,
        up_mask.T,
        down_mask,
        gate_weight,
        up_weight,
        down_weight,
    )
    return out.reshape(blocks, 2, LANES).transpose(1, 0, 2).reshape(own, feats)


def solution(mesh):
    return jax.shard_map(
        functools.partial(local, mesh.shape["blk"]),
        mesh=mesh,
        in_specs=(
            P(("blk", "rows"), None),
            P(),
            P(None, "blk"),
            P(None, "blk"),
            P("blk", None),
            P(None, "blk"),
            P(None, "blk"),
            P("blk", None),
        ),
        out_specs=P(("blk", "rows"), None),
        check_vma=False,
    )
```

```python
import functools

import jax
import jax.numpy as jnp
from jax import lax
from jax.experimental import pallas as pl
from jax.experimental.pallas import tpu as pltpu
from jax.sharding import PartitionSpec as P

MESH = pl.DeviceIdType.MESH
F32 = jnp.float32
BF16 = jnp.bfloat16
LANES = 128
CUT = 1024
GROUP = 16


def permutation(to_tokens):
    size = GROUP * 16
    row = lax.broadcasted_iota(jnp.int32, (size, size), 0)
    col = lax.broadcasted_iota(jnp.int32, (size, size), 1)
    if not to_tokens:
        row, col = col, row
    block, device, token = row >> 5, (row & 31) >> 1, row & 1
    return jnp.where(device * 16 + block * 2 + token == col, 1.0, 0.0).astype(BF16)


def kernel(
    nblk,
    tok_hbm,
    gain_hbm,
    gm_hbm,
    um_hbm,
    dm_hbm,
    wg_hbm,
    wu_hbm,
    wd_hbm,
    out_ref,
    tok_ref,
    gain_ref,
    gm_ref,
    um_ref,
    dm_ref,
    wg,
    wu,
    wd,
    wide,
    slabs,
    x,
    swap_out,
    swap_in,
    rs_out,
    rs_in,
    fin_out,
    fin_in,
    s_sem,
    w_sem,
    ag_send,
    by_send,
    fw_send,
    ag_recv,
    swap_send,
    swap_recv,
    rs_send,
    rs_recv,
    fin_send,
    fin_recv,
):
    nchips = nblk // 2
    feats = wg.shape[0]
    hid = wg.shape[1]
    blocks = feats // LANES
    cuts = feats // CUT
    half_cuts = cuts // 2
    rows_half = blocks
    groups = nblk // GROUP
    me = lax.axis_index("blk")
    chip, core = me // 2, me % 2
    sib = chip * 2 + (1 - core)

    def peer(o):
        return lax.rem(chip + o, nchips)

    smalls = [
        pltpu.make_async_copy(a, b, s_sem.at[n])
        for n, (a, b) in enumerate(
            (
                (tok_hbm, tok_ref),
                (gain_hbm, gain_ref),
                (gm_hbm, gm_ref),
                (um_hbm, um_ref),
                (dm_hbm, dm_ref),
            )
        )
    ]
    for a in smalls:
        a.start()

    loads = []
    for n in range(4):
        r = feats // 4
        rs = pl.ds(n * r, r)
        loads.append(
            (
                pltpu.make_async_copy(wg_hbm.at[rs], wg.at[rs], w_sem.at[0, n]),
                pltpu.make_async_copy(wu_hbm.at[rs], wu.at[rs], w_sem.at[1, n]),
            )
        )
    down_loads = []
    for n in range(4):
        r = feats // 4
        cs = pl.ds(n * r, r)
        down_loads.append(pltpu.make_async_copy(wd_hbm.at[:, cs], wd.at[:, cs], w_sem.at[2, n]))
    for a, b in loads:
        a.start()
        b.start()
    for a in down_loads:
        a.start()

    barrier = pltpu.get_barrier_semaphore()
    pl.semaphore_signal(barrier, inc=1, device_id={"blk": sib}, device_id_type=MESH)

    def greet(o, c):
        pl.semaphore_signal(barrier, inc=1, device_id={"blk": peer(o) * 2 + core}, device_id_type=MESH)
        return c

    lax.fori_loop(1, nchips, greet, 0)

    smalls[0].wait()
    smalls[1].wait()
    tok = tok_ref[...].astype(F32)
    inv = lax.rsqrt(jnp.mean(tok * tok, axis=-1, keepdims=True) + 1e-05)
    normed = tok * inv * gain_ref[...]
    for b in range(blocks):
        wide[pl.ds(2 * b, 2), :] = normed[:, b * LANES : (b + 1) * LANES]
    slabs[me] = wide[...].astype(BF16)

    pl.semaphore_wait(barrier, nchips)

    def ag_copy(src, dev, send):
        return pltpu.make_async_remote_copy(
            src_ref=slabs.at[src],
            dst_ref=slabs.at[src],
            send_sem=send,
            recv_sem=ag_recv.at[src],
            device_id={"blk": dev},
            device_id_type=MESH,
        )

    pairs = nchips // 2
    pair, side = chip // 2, chip % 2
    beside = (pair * 2 + (1 - side)) * 2 + core

    def slab_of(o, s, c):
        return (lax.rem(pair + pairs - o, pairs) * 2 + s) * 2 + c

    def send_all(o, c):
        ag_copy(me, (lax.rem(pair + o, pairs) * 2 + side) * 2 + core, ag_send.at[o]).start()
        return c

    lax.fori_loop(1, pairs, send_all, 0)
    ag_copy(me, beside, by_send.at[0]).start()
    ag_copy(me, sib, fw_send.at[0, 0]).start()
    for a in smalls[2:]:
        a.wait()

    def forward_both(o, c):
        src = slab_of(o, side, core)
        ag_copy(src, sib, fw_send.at[0, o]).wait_recv()
        ag_copy(src, beside, by_send.at[o]).start()
        ag_copy(src, sib, fw_send.at[0, o]).start()
        return c

    def forward_last(o, c):
        src = slab_of(o, 1 - side, core)
        ag_copy(src, sib, fw_send.at[1, o]).wait_recv()
        ag_copy(src, sib, fw_send.at[1, o]).start()
        return c

    def flagged(w, flag):
        keep = jnp.broadcast_to(flag.astype(F32), (16, LANES)).astype(BF16)
        return (w.reshape(8, 16, LANES) * keep[None]).reshape(LANES, LANES)

    per = blocks // 4
    for n in range(4):
        loads[n][0].wait()
        loads[n][1].wait()

        def mask_in(i, c):
            i = n * per + i
            rs = pl.ds(pl.multiple_of(i * LANES, LANES), LANES)
            for j in range(hid // LANES):
                cs = pl.ds(j * LANES, LANES)
                wg[rs, cs] = flagged(wg[rs, cs], gm_ref[j, i])
                wu[rs, cs] = flagged(wu[rs, cs], um_ref[j, i])
            return c

        lax.fori_loop(0, per, mask_in, 0, unroll=4)
        lax.fori_loop(1 + (pairs - 1) * n // 4, 1 + (pairs - 1) * (n + 1) // 4, forward_both, 0)

    for n in range(4):
        down_loads[n].wait()

        def mask_down(i, c):
            i = n * per + i
            cs = pl.ds(pl.multiple_of(i * LANES, LANES), LANES)
            for j in range(hid // LANES):
                rs = pl.ds(j * LANES, LANES)
                wd[rs, cs] = flagged(wd[rs, cs], dm_ref[j, i])
            return c

        lax.fori_loop(0, per, mask_down, 0, unroll=4)
        lax.fori_loop(pairs * n // 4, pairs * (n + 1) // 4, forward_last, 0)

    def arrived(o, c):
        src = lax.rem(chip + nchips - o, nchips) * 2 + (1 - core)
        ag_copy(src, sib, fw_send.at[0, 0]).wait_recv()
        return c

    lax.fori_loop(0, nchips, arrived, 0)

    to_tokens = permutation(True)
    gate = jnp.zeros((2 * nblk, hid), F32)
    up = jnp.zeros((2 * nblk, hid), F32)
    for n in range(cuts):
        for g in range(groups):
            part = slabs[pl.ds(g * GROUP, GROUP), pl.ds(n * 16, 16), :].reshape(GROUP * 16, LANES)
            turned = jnp.dot(to_tokens, part, preferred_element_type=F32).astype(BF16)
            for b in range(8):
                x[pl.ds(g * 32, 32), pl.ds(b * LANES, LANES)] = turned[b * 32 : (b + 1) * 32]
        rs = pl.ds(n * CUT, CUT)
        gate = gate + jnp.dot(x[...], wg[rs, :], preferred_element_type=F32)
        up = up + jnp.dot(x[...], wu[rs, :], preferred_element_type=F32)
    hidden = (gate / (1.0 + jnp.exp(-gate)) * up).astype(BF16)

    def swap_copy(n):
        cs = pl.ds(n * CUT, CUT)
        return pltpu.make_async_remote_copy(
            src_ref=swap_out.at[:, cs],
            dst_ref=swap_in.at[:, cs],
            send_sem=swap_send.at[n],
            recv_sem=swap_recv.at[n],
            device_id={"blk": sib},
            device_id_type=MESH,
        )

    for n in range(half_cuts):
        at = pl.multiple_of(((1 - core) * half_cuts + n) * CUT, CUT)
        part = jnp.dot(hidden, wd[:, pl.ds(at, CUT)], preferred_element_type=F32)
        swap_out[:, pl.ds(n * CUT, CUT)] = part.astype(BF16)
        swap_copy(n).start()

    def rs_copy(src, dst, o, dev, n):
        rows = pl.ds(n * 16, 16)
        return pltpu.make_async_remote_copy(
            src_ref=rs_out.at[src, :, rows],
            dst_ref=rs_in.at[dst, :, rows],
            send_sem=rs_send.at[o, n],
            recv_sem=rs_recv.at[dst, n],
            device_id={"blk": dev},
            device_id_type=MESH,
        )

    to_slabs = permutation(False)
    for n in range(half_cuts):
        at = pl.multiple_of((core * half_cuts + n) * CUT, CUT)
        part = jnp.dot(hidden, wd[:, pl.ds(at, CUT)], preferred_element_type=F32)
        swap_copy(n).wait_recv()
        both = (part + swap_in[:, pl.ds(n * CUT, CUT)].astype(F32)).astype(BF16)
        for g in range(groups):
            mine = both[g * 32 : (g + 1) * 32]
            stacked = jnp.concatenate([mine[:, b * LANES : (b + 1) * LANES] for b in range(8)], axis=0)
            turned = jnp.dot(to_slabs, stacked, preferred_element_type=F32).astype(BF16)
            rs_out[pl.ds(g * GROUP // 2, GROUP // 2), :, pl.ds(n * 16, 16), :] = turned.reshape(
                GROUP // 2, 2, 16, LANES
            )

        def rs_start(o, c):
            to = peer(o)
            rs_copy(to, chip, o, to * 2 + core, n).start()
            return c

        lax.fori_loop(1, nchips, rs_start, 0)

    def rs_add(o, total):
        src = lax.rem(chip + nchips - o, nchips)
        for n in range(half_cuts):
            rs_copy(src, src, o, src * 2 + core, n).wait_recv()
        return total + rs_in[src].astype(F32)

    total = lax.fori_loop(1, nchips, rs_add, rs_out[chip].astype(F32))
    fin_out[...] = total.astype(BF16)
    fin = pltpu.make_async_remote_copy(
        src_ref=fin_out.at[1 - core],
        dst_ref=fin_in,
        send_sem=fin_send,
        recv_sem=fin_recv,
        device_id={"blk": sib},
        device_id_type=MESH,
    )
    fin.start()
    out_ref[core] = fin_out[core]

    def drain_own(o, c):
        ag_copy(me, sib, ag_send.at[o]).wait_send()
        return c

    def drain_forwards(o, c):
        ag_copy(me, sib, by_send.at[o]).wait_send()
        ag_copy(me, sib, fw_send.at[0, o]).wait_send()
        ag_copy(me, sib, fw_send.at[1, o]).wait_send()
        return c

    def drain_sums(o, c):
        for n in range(half_cuts):
            rs_copy(chip, chip, o, sib, n).wait_send()
        return c

    lax.fori_loop(1, pairs, drain_own, 0)
    lax.fori_loop(0, pairs, drain_forwards, 0)
    lax.fori_loop(1, nchips, drain_sums, 0)
    for n in range(half_cuts):
        swap_copy(n).wait_send()
    fin.wait()
    out_ref[1 - core] = fin_in[...]


def local(nblk, tokens, norm_gain, gate_weight, up_weight, down_weight, gate_mask, up_mask, down_mask):
    own, feats = tokens.shape
    hid = gate_weight.shape[1]
    blocks = feats // LANES
    half = feats // 2
    nchips = nblk // 2
    cuts = half // CUT
    vmem = pl.BlockSpec(memory_space=pltpu.VMEM)
    held = pl.BlockSpec(memory_space=pltpu.HBM)
    anyw = pl.BlockSpec(memory_space=pl.ANY)
    dma = pltpu.SemaphoreType.DMA
    out = pl.pallas_call(
        functools.partial(kernel, nblk),
        out_shape=jax.ShapeDtypeStruct((2, blocks, LANES), BF16),
        in_specs=[held] * 5 + [anyw] * 3,
        out_specs=vmem,
        scratch_shapes=[
            pltpu.VMEM((own, feats), BF16),
            pltpu.VMEM((1, feats), F32),
            pltpu.SMEM((hid // LANES, blocks), jnp.int32),
            pltpu.SMEM((hid // LANES, blocks), jnp.int32),
            pltpu.SMEM((hid // LANES, blocks), jnp.int32),
            pltpu.VMEM((feats, hid), BF16),
            pltpu.VMEM((feats, hid), BF16),
            pltpu.VMEM((hid, feats), BF16),
            pltpu.VMEM((2 * blocks, LANES), F32),
            pltpu.VMEM((nblk, 2 * blocks, LANES), BF16),
            pltpu.VMEM((2 * nblk, CUT), BF16),
            pltpu.VMEM((2 * nblk, half), BF16),
            pltpu.VMEM((2 * nblk, half), BF16),
            pltpu.VMEM((nchips, 2, blocks, LANES), BF16),
            pltpu.VMEM((nchips, 2, blocks, LANES), BF16),
            pltpu.VMEM((2, blocks, LANES), BF16),
            pltpu.VMEM((blocks, LANES), BF16),
            dma((5,)),
            dma((3, 4)),
            dma((nchips // 2,)),
            dma((nchips // 2,)),
            dma((2, nchips // 2)),
            dma((nblk,)),
            dma((cuts,)),
            dma((cuts,)),
            dma((nchips, cuts)),
            dma((nchips, cuts)),
            dma,
            dma,
        ],
        compiler_params=pltpu.CompilerParams(
            collective_id=0, has_side_effects=True, vmem_limit_bytes=64 * 1024 * 1024 - 65536
        ),
    )(
        tokens,
        norm_gain.reshape(1, feats),
        gate_mask.T,
        up_mask.T,
        down_mask,
        gate_weight,
        up_weight,
        down_weight,
    )
    return out.reshape(blocks, 2, LANES).transpose(1, 0, 2).reshape(own, feats)


def solution(mesh):
    return jax.shard_map(
        functools.partial(local, mesh.shape["blk"]),
        mesh=mesh,
        in_specs=(
            P(("blk", "rows"), None),
            P(),
            P(None, "blk"),
            P(None, "blk"),
            P("blk", None),
            P(None, "blk"),
            P(None, "blk"),
            P("blk", None),
        ),
        out_specs=P(("blk", "rows"), None),
        check_vma=False,
    )
```
